32 devices in a mesh: expert: 8 (over y, x, core), dp: 4 (over z).
Axes of the slice: x: 2, y: 2, z: 4, core: 2. Of those that a mesh axis runs over, the one named last changes fastest.
Arguments:
- tokens: bfloat16 [4096, 2048], P(('expert', 'dp')), may hold values from -6 to 6
- cotangent: bfloat16 [4096, 2048], P(('expert', 'dp')), may hold values from -4 to 4
- expert_ids: int32 [4096, 8], P('expert'), may hold values from 0 to 31, all different within a row; in each aligned block of 512 rows (0 to 511, 512 to 1023, ...) at most 160 rows name the same one
- router_probs: float32 [4096, 8], P('expert'), may hold values from 0.02 to 1
- w_gate: bfloat16 [32, 2048, 768], P(('expert', 'dp')), may hold values from -0.125 to 0.125
- w_up: bfloat16 [32, 2048, 768], P(('expert', 'dp')), may hold values from -0.125 to 0.125
- w_down: bfloat16 [32, 768, 2048], P(('expert', 'dp')), may hold values from -0.21875 to 0.21875
Outputs:
- moe_out: bfloat16 [4096, 2048], P(('expert', 'dp'))
- token_grad: bfloat16 [4096, 2048], P(('expert', 'dp'))
- prob_grad: float32 [4096, 8], P(('expert', 'dp'))
The draws below stay inside these ranges and needn't reach their ends.
Inputs may be any that keep to these rules, and one draw needn't show every extreme that they name: `expert_ids`: each row names 8 different experts. In each aligned block of 512 rows (the tokens of one index of expert) no expert is named by more than 160 rows, and in some block one expert is named by exactly 160 rows.
All inputs are finite; a program needn't handle non-finite values.
Results may differ from the reference program's by a relative error of at most 0.0095.
Values may be sent and summed in bfloat16 or wider, within the bound.
A program may use at most 128 MiB of HBM per device.

```python
import math
import jax
import jax.numpy as jnp
import numpy as np
from jax import lax

D = 2048
FF = 768
TOPK = 8
GROUPS = 4
COL_TOK = 512
TOKENS = 4096
EXPERTS = 32
CAP = 160
N_EXPERT = 8


def block_scale(key, shape, pieces, smallest, top_value):
    gain, own = 1.0, jax.random.fold_in(key, 6)
    for dim, blocks in pieces:
        steps = jnp.exp(jax.random.uniform(jax.random.fold_in(own, dim), (blocks,), jnp.float32, smallest / len(pieces), top_value / len(pieces)))
        gain = gain * jnp.repeat(steps, shape[dim] // blocks).reshape([-1 if axis == dim else 1 for axis in range(len(shape))])
    return gain


def assign_block(own_key, own, number, rows, amount, top, limit, skew):
    order = jax.random.permutation(own_key, amount)
    packed, ordinary = load_shares(amount, rows * top, limit, skew, True), load_shares(amount, rows * top, limit, skew, False)
    places = jnp.arange(amount)

    def named(tallies, rotation):
        used = int((tallies > 0).sum())
        fixed = max(1, used // 4)
        passed = fixed + (places - fixed + rotation * (used - fixed)) % max(1, amount - fixed)
        return jnp.zeros((amount,), jnp.int32).at[order[jnp.where(places < fixed, places, passed)]].set(jnp.asarray(tallies, jnp.int32))

    tallies = jnp.where(number % 4 == 0, named(packed, number // 4), named(ordinary, number - number // 4 - 1))
    mixed = jax.random.permutation(jax.random.fold_in(own, 3), amount)
    giver, receiver = mixed[0:amount // 2 * 2:2], mixed[1:amount // 2 * 2:2]
    room = jnp.minimum(tallies[giver] - 1, limit - tallies[receiver]) // 2
    room = jnp.where((giver == order[0]) | (receiver == order[0]) | (tallies[receiver] == 0), 0, jnp.maximum(room, 0))
    passed = jax.random.randint(jax.random.fold_in(own, 4), (amount // 2,), 0, 1 << 20) % (room + 1)
    tallies = tallies.at[giver].add(-passed).at[receiver].add(passed)
    members = jnp.searchsorted(jnp.cumsum(tallies), jnp.arange(rows * top), side="right").astype(jnp.int32)
    table = members.reshape(top, rows).T
    table = table[jax.random.permutation(jax.random.fold_in(own, 1), rows)]
    rotation = jax.random.randint(jax.random.fold_in(own, 2), (rows, 1), 0, top)
    return jnp.take_along_axis(table, (jnp.arange(top)[None, :] + rotation) % top, axis=1)


def load_shares(number_of, total, limit, skew, full):
    portions = [(1 << 20) // math.isqrt(rank ** skew) + 1 for rank in range(1, number_of + 1)]
    largest = limit if full else min(limit, max(-(-total // number_of), total * portions[0] // sum(portions)))
    least = 1 if total - largest >= number_of - 1 else 0
    holding, spare = [largest] + [least] * (number_of - 1), total - largest - least * (number_of - 1)
    while spare > 0:
        free = [i for i in range(1, number_of) if holding[i] < largest] or [i for i in range(1, number_of) if holding[i] < limit]
        pool, budget = sum([portions[i] for i in free]), spare
        for i in free:
            extra = min(limit - holding[i], max(1, budget * portions[i] // pool), spare)
            holding[i] = holding[i] + extra
            spare = spare - extra
    return np.array(holding)


def centred(rng, extent, spread, most, pieces=(), held_as=jnp.bfloat16):
    result = jax.random.normal(rng, extent, jnp.float32) * spread
    if len(pieces) > 0:
        result = block_scale(rng, extent, pieces, -0.22, 0.18) * result
    return jnp.clip(result, min=-most, max=most).astype(held_as)


def setup_inputs(seed: int = 0) -> dict:
    key_list = jax.random.split(jax.random.key(seed), 8)
    tokens = centred(key_list[0], (TOKENS, D), 1.0, 6.0, ((0, 32),))
    cotangent = centred(key_list[1], (TOKENS, D), 0.5, 4.0, ((0, 32),))
    expert_ids_keys = jax.random.split(jax.random.fold_in(key_list[2], 1), TOKENS // COL_TOK)
    expert_ids_turns = jax.random.permutation(jax.random.fold_in(key_list[2], 3), TOKENS // COL_TOK)
    expert_ids = jax.vmap(lambda own, number: assign_block(jax.random.fold_in(key_list[2], 2), own, number, COL_TOK, EXPERTS, TOPK, CAP, 2))(expert_ids_keys, expert_ids_turns).reshape((TOKENS, TOPK))
    router_probs = jnp.clip(jnp.exp(math.log(1.0) - 3.912023 * jax.random.uniform(key_list[3], (TOKENS, TOPK), jnp.float32) ** block_scale(key_list[3], (TOKENS, TOPK), ((0, 8),), -0.2, 0.2)), 0.02, 1.0)
    w_gate = centred(key_list[4], (EXPERTS, D, FF), D ** -0.5, 0.125, ((0, 32),))
    w_up = centred(key_list[5], (EXPERTS, D, FF), D ** -0.5, 0.125, ((0, 32),))
    w_down = centred(key_list[6], (EXPERTS, FF, D), FF ** -0.5, 0.21875, ((0, 32),))
    return {"tokens": tokens, "cotangent": cotangent, "expert_ids": expert_ids, "router_probs": router_probs, "w_gate": w_gate, "w_up": w_up, "w_down": w_down}


def rounded(values):
    return lax.optimization_barrier(values.astype(jnp.bfloat16)).astype(jnp.float32)


def expert_block(expert_num, tokens, cotangent, expert_flat, weight_flat, w_gate, w_up, w_down):
    rows_max = N_EXPERT * CAP
    flat_count = expert_flat.shape[0]
    is_expert = expert_flat == expert_num
    position = jnp.cumsum(is_expert.astype(jnp.int32), dtype=jnp.int32) - 1
    target = jnp.where(is_expert, position, rows_max).astype(jnp.int32)
    slot_row = jnp.zeros((rows_max + 1,), jnp.int32).at[target].set(jnp.arange(flat_count, dtype=jnp.int32))[:rows_max]
    filled = jnp.zeros((rows_max + 1,), jnp.float32).at[target].set(1.0)[:rows_max]
    slot_token = slot_row // TOPK
    slot_weight = weight_flat[slot_row] * filled
    gate_matrix = w_gate[expert_num]
    up_matrix = w_up[expert_num]
    down_matrix = w_down[expert_num]
    token_rows = jnp.where(filled[:, None] > 0, tokens[slot_token], jnp.zeros((), jnp.bfloat16))
    gate_pre = jnp.dot(token_rows, gate_matrix, preferred_element_type=jnp.float32)
    up_pre = jnp.dot(token_rows, up_matrix, preferred_element_type=jnp.float32)
    hidden = (jax.nn.silu(gate_pre) * up_pre).astype(jnp.bfloat16)
    expert_out = jnp.dot(hidden, down_matrix, preferred_element_type=jnp.float32).astype(jnp.bfloat16)
    cot_tokens = cotangent[slot_token]
    cot_rows = (slot_weight[:, None] * cot_tokens.astype(jnp.float32)).astype(jnp.bfloat16)
    hidden_grad = lax.dot_general(cot_rows, down_matrix, (((1,), (1,)), ((), ())), preferred_element_type=jnp.float32)
    sigmoid_gate = jax.nn.sigmoid(gate_pre)
    gate_grad = (hidden_grad * up_pre * sigmoid_gate * (1.0 + gate_pre * (1.0 - sigmoid_gate))).astype(jnp.bfloat16)
    up_grad = (hidden_grad * gate_pre * sigmoid_gate).astype(jnp.bfloat16)
    input_rows = lax.dot_general(gate_grad, gate_matrix, (((1,), (1,)), ((), ())), preferred_element_type=jnp.float32)
    input_rows = input_rows + lax.dot_general(up_grad, up_matrix, (((1,), (1,)), ((), ())), preferred_element_type=jnp.float32)
    input_rows = input_rows.astype(jnp.bfloat16)
    slot_grad = jnp.sum(cot_tokens.astype(jnp.float32) * expert_out.astype(jnp.float32), axis=1)
    return slot_token, slot_row, slot_weight, expert_out, input_rows, slot_grad


def reference(tokens, cotangent, expert_ids, router_probs, w_gate, w_up, w_down):
    prob_total = jnp.sum(router_probs, axis=1, keepdims=True)
    weights = router_probs / prob_total
    expert_flat = expert_ids.reshape(-1)
    weight_flat = weights.reshape(-1)
    out_total = jnp.zeros((TOKENS, D), jnp.float32)
    grad_total = jnp.zeros((TOKENS, D), jnp.float32)
    slot_total = jnp.zeros((TOKENS * TOPK,), jnp.float32)
    for group_num in range(GROUPS):
        def per_expert(carry, column_num):
            out_part, grad_part, slot_part = carry
            expert_num = (column_num * GROUPS + group_num).astype(jnp.int32)
            slot_token, slot_row, slot_weight, expert_out, input_rows, slot_grad = expert_block(
                expert_num, tokens, cotangent, expert_flat, weight_flat, w_gate, w_up, w_down)
            out_part = out_part.at[slot_token].add(slot_weight[:, None] * expert_out.astype(jnp.float32))
            grad_part = grad_part.at[slot_token].add(input_rows.astype(jnp.float32))
            slot_part = slot_part.at[slot_row].add(slot_grad)
            return (out_part, grad_part, slot_part), None

        start = (jnp.zeros((TOKENS, D), jnp.float32), jnp.zeros((TOKENS, D), jnp.float32), jnp.zeros((TOKENS * TOPK,), jnp.float32))
        (out_part, grad_part, slot_part), _ = lax.scan(per_expert, start, jnp.arange(N_EXPERT, dtype=jnp.int32))
        out_total = out_total + rounded(out_part)
        grad_total = grad_total + rounded(grad_part)
        slot_total = slot_total + rounded(slot_part)
    slot_grad = slot_total.reshape(TOKENS, TOPK)
    prob_grad = (slot_grad - jnp.sum(weights * slot_grad, axis=1, keepdims=True)) / prob_total
    return (out_total.astype(jnp.bfloat16), grad_total.astype(jnp.bfloat16), prob_grad)
```

```python
import jax
import jax.numpy as jnp
from jax import lax
from jax.sharding import PartitionSpec as P

BF = jnp.bfloat16
F32 = jnp.float32
PIECES = 2
NT = (((1,), (1,)), ((), ()))


def shards(tokens, cotangent, expert_ids, router_probs, w_gate, w_up, w_down):
    cols = lax.axis_size("expert")
    groups = lax.axis_size("dp")
    group = lax.axis_index("dp")
    own, width = tokens.shape
    col_tok, top = expert_ids.shape
    capacity = col_tok * top * 5 // (4 * cols * groups)
    piece = width // PIECES
    cuts = [slice(h * piece, (h + 1) * piece) for h in range(PIECES)]

    def exchange(rows):
        return lax.all_to_all(rows, "expert", split_axis=0, concat_axis=0, tiled=True)

    def gather(rows):
        return lax.all_gather(rows, "dp", axis=0, tiled=True)

    def scatter(rows):
        return lax.psum_scatter(rows, "dp", scatter_dimension=0, tiled=True)

    tok_col = [gather(tokens[:, s]) for s in cuts]
    cot_col = [gather(cotangent[:, s]) for s in cuts]

    weights = router_probs / jnp.sum(router_probs, axis=1, keepdims=True)
    experts = jnp.arange(cols, dtype=jnp.int32) * groups + group
    named = expert_ids[None, :, :] == experts[:, None, None]
    hit = jnp.any(named, axis=2)
    slot_w = jnp.sum(jnp.where(named, weights[None], 0.0), axis=2)
    step = jnp.arange(col_tok, dtype=jnp.int32)
    before = (step[:, None] < step[None, :]).astype(BF)
    place = jnp.dot(hit.astype(BF), before, preferred_element_type=F32).astype(jnp.int32)
    place = jnp.where(hit, place, -1)
    pick = place[:, None, :] == jnp.arange(capacity, dtype=jnp.int32)[None, :, None]
    row_w = jnp.sum(jnp.where(pick, slot_w[:, None, :], 0.0), axis=2).reshape(-1, 1)
    pick_w = jnp.where(pick, slot_w[:, None, :], 0.0).astype(BF).reshape(cols * capacity, col_tok)
    pick = pick.astype(BF).reshape(cols * capacity, col_tok)

    def select(rows):
        return jnp.dot(pick, rows, preferred_element_type=F32).astype(BF)

    def send(rows):
        return exchange(rows.reshape(cols, capacity, -1)).reshape(cols * capacity, -1)

    def combine(matrix, rows):
        return lax.dot_general(
            matrix, rows, (((0,), (0,)), ((), ())), preferred_element_type=F32
        ).astype(BF)

    gate_m, up_m, down_m = w_gate[0], w_up[0], w_down[0]
    x = [send(select(c)) for c in tok_col]
    cot_sel = [select(c) for c in cot_col]
    cot = [send((row_w * c.astype(F32)).astype(BF)) for c in cot_sel]

    gate = sum(jnp.dot(r, gate_m[s], preferred_element_type=F32) for r, s in zip(x, cuts))
    up = sum(jnp.dot(r, up_m[s], preferred_element_type=F32) for r, s in zip(x, cuts))
    sig = jax.nn.sigmoid(gate)
    hidden = (gate * sig * up).astype(BF)
    back = [
        send(jnp.dot(hidden, down_m[:, s], preferred_element_type=F32).astype(BF)) for s in cuts
    ]
    out_sum = jnp.concatenate([scatter(combine(pick_w, b)) for b in back], axis=1)

    hg = sum(
        lax.dot_general(r, down_m[:, s], NT, preferred_element_type=F32) for r, s in zip(cot, cuts)
    )
    gate_grad = (hg * up * sig * (1.0 + gate * (1.0 - sig))).astype(BF)
    up_grad = (hg * gate * sig).astype(BF)

    slot_g = sum(
        jnp.sum(c.astype(F32) * b.astype(F32), axis=1) for c, b in zip(cot_sel, back)
    ).reshape(cols, capacity)
    slot_t = jnp.sum(
        jnp.where(pick.reshape(cols, capacity, col_tok) > 0, slot_g[:, :, None], 0.0), axis=1
    )
    slot_tk = jnp.sum(jnp.where(named, slot_t[:, :, None], 0.0), axis=0)
    slot_sum = scatter(slot_tk.astype(BF)).astype(F32)

    grads = [
        send(
            (
                lax.dot_general(gate_grad, gate_m[s], NT, preferred_element_type=F32)
                + lax.dot_general(up_grad, up_m[s], NT, preferred_element_type=F32)
            ).astype(BF)
        )
        for s in cuts
    ]
    grad_sum = jnp.concatenate([scatter(combine(pick, g)) for g in grads], axis=1)

    own_probs = lax.dynamic_slice_in_dim(router_probs, group * own, own, 0)
    own_total = jnp.sum(own_probs, axis=1, keepdims=True)
    own_w = own_probs / own_total
    prob_grad = (slot_sum - jnp.sum(own_w * slot_sum, axis=1, keepdims=True)) / own_total
    return out_sum, grad_sum, prob_grad


def solution(mesh):
    rows = P(("expert", "dp"), None)
    mats = P(("expert", "dp"), None, None)
    return jax.shard_map(
        shards,
        mesh=mesh,
        in_specs=(rows, rows, P("expert", None), P("expert", None), mats, mats, mats),
        out_specs=(rows, rows, rows),
        check_vma=False,
    )
```

```python
import functools

import jax
import jax.numpy as jnp
from jax import lax
from jax.experimental import pallas as pl
from jax.experimental.pallas import tpu as pltpu
from jax.sharding import PartitionSpec as P

BF = jnp.bfloat16
F32 = jnp.float32
PIECES = 2
NT = (((1,), (1,)), ((), ()))
CHUNKS = 4
VMEM_BYTES = 60 * 1024 * 1024
MESH = pl.DeviceIdType.MESH


def layer_kernel(
    cols, groups, tok_ref, cot_ref, pick_ref, pick_t_ref, pick_wt_ref, row_w_ref, kinv_ref,
    gate_ref, up_ref, down_ref, out_ref, grad_ref, slot_ref,
    tok_col, cot_col, send_tok, recv_tok, send_cot, recv_cot, ret_out, gate_keep, up_keep,
    slot_rows, slot_col, rs_out, rs_grad, rs_slot,
    zsend, zrecv, ssend, srecv, osend, orecv, gsend, grecv, rsend, rrecv,
):
    me = lax.axis_index("expert")
    z = lax.axis_index("dp")
    own, width = tok_ref.shape
    cap = pick_ref.shape[0] // cols
    part = width // CHUNKS
    cuts = [slice(c * part, (c + 1) * part) for c in range(CHUNKS)]
    whole = slice(0, width)

    def block(index, size):
        return pl.ds(pl.multiple_of(index * size, 16), size)

    def peer(j):
        return lax.rem(me + j, cols)

    def zpeer(j):
        return lax.rem(z + j, groups)

    def loop(start, stop, body):
        def step(j, carry):
            body(j)
            return carry
        lax.fori_loop(start, stop, step, 0)

    def remote(src, dst, send, recv, device):
        return pltpu.make_async_remote_copy(
            src_ref=src, dst_ref=dst, send_sem=send, recv_sem=recv,
            device_id=device, device_id_type=MESH,
        )

    barrier = pltpu.get_barrier_semaphore()
    loop(1, cols, lambda j: pl.semaphore_signal(
        barrier, inc=1, device_id=(peer(j), z), device_id_type=MESH))
    loop(1, groups, lambda j: pl.semaphore_signal(
        barrier, inc=1, device_id=(me, zpeer(j)), device_id_type=MESH))
    pl.semaphore_wait(barrier, cols + groups - 2)

    def zcopy(k, c, src_z, to):
        src = (tok_ref, cot_ref)[k]
        dst = (tok_col, cot_col)[k]
        return remote(src.at[:, cuts[c]], dst.at[block(src_z, own), cuts[c]],
                      zsend.at[k, c, to], zrecv.at[k, c, src_z], (me, to))

    for k in range(2):
        for c in range(CHUNKS):
            loop(1, groups, lambda j, k=k, c=c: zcopy(k, c, z, zpeer(j)).start())
    tok_col[block(z, own), :] = tok_ref[...]
    cot_col[block(z, own), :] = cot_ref[...]

    def row_copy(k, c, src, to):
        a = (send_tok, send_cot)[k]
        b = (recv_tok, recv_cot)[k]
        return remote(a.at[block(to, cap), cuts[c]], b.at[block(src, cap), cuts[c]],
                      ssend.at[k, c, to], srecv.at[k, c, src], (to, z))

    for k in range(2):
        for c in range(CHUNKS):
            loop(1, groups, lambda j, k=k, c=c: zcopy(k, c, zpeer(j), zpeer(j)).wait_recv())

            def picked(d, k=k, c=c):
                col = (tok_col, cot_col)[k]
                rows = jnp.dot(pick_ref[block(d, cap), :], col[:, cuts[c]],
                               preferred_element_type=F32)
                if k == 1:
                    rows = rows * row_w_ref[block(d, cap), :]
                return rows.astype(BF)

            def dispatch(j, k=k, c=c):
                d = peer(j)
                (send_tok, send_cot)[k][block(d, cap), cuts[c]] = picked(d)
                if k == 1:
                    row_copy(0, c, me, d).wait_send()
                row_copy(k, c, me, d).start()

            loop(1, cols, dispatch)
            mine = picked(me)
            (recv_tok, recv_cot)[k][block(me, cap), cuts[c]] = mine
            if k == 1:
                send_cot[block(me, cap), cuts[c]] = mine
    for k in range(2):
        for c in range(CHUNKS):
            loop(1, groups, lambda j, k=k, c=c: zcopy(k, c, z, zpeer(j)).wait_send())

    def out_copy(src, to):
        return remote(recv_tok.at[block(to, cap), :], ret_out.at[block(src, cap), :],
                      osend.at[to], orecv.at[src], (to, z))

    def forward(s):
        rows = block(s, cap)
        x = recv_tok[rows, :]
        gate = jnp.dot(x, gate_ref[...], preferred_element_type=F32)
        up = jnp.dot(x, up_ref[...], preferred_element_type=F32)
        gate_keep[rows, :] = gate.astype(BF)
        up_keep[rows, :] = up.astype(BF)
        hidden = (gate * jax.nn.sigmoid(gate) * up).astype(BF)
        return jnp.dot(hidden, down_ref[...], preferred_element_type=F32).astype(BF)

    ret_out[block(me, cap), :] = forward(me)

    def forward_step(j):
        s = peer(cols - j)
        for c in range(CHUNKS):
            row_copy(0, c, s, s).wait_recv()
        recv_tok[block(s, cap), :] = forward(s)
        out_copy(me, s).start()

    loop(1, cols, forward_step)

    def backward(s):
        rows = block(s, cap)
        hg = lax.dot_general(recv_cot[rows, :], down_ref[...], NT, preferred_element_type=F32)
        gate = gate_keep[rows, :].astype(F32)
        up = up_keep[rows, :].astype(F32)
        sig = jax.nn.sigmoid(gate)
        gate_keep[rows, :] = (hg * up * sig * (1.0 + gate * (1.0 - sig))).astype(BF)
        up_keep[rows, :] = (hg * gate * sig).astype(BF)

    backward(me)

    def backward_step(j):
        s = peer(cols - j)
        for c in range(CHUNKS):
            row_copy(1, c, s, s).wait_recv()
        backward(s)

    loop(1, cols, backward_step)

    def grad_copy(c, src, to):
        return remote(recv_cot.at[block(to, cap), cuts[c]], send_tok.at[block(src, cap), cuts[c]],
                      gsend.at[c, to], grecv.at[c, src], (to, z))

    def grad_rows(s, c):
        rows = block(s, cap)
        return (
            lax.dot_general(gate_keep[rows, :], gate_ref[cuts[c], :], NT,
                            preferred_element_type=F32)
            + lax.dot_general(up_keep[rows, :], up_ref[cuts[c], :], NT,
                              preferred_element_type=F32)
        ).astype(BF)

    for c in range(CHUNKS):
        def grad_step(j, c=c):
            s = peer(cols - j)
            recv_cot[block(s, cap), cuts[c]] = grad_rows(s, c)
            grad_copy(c, me, s).start()

        loop(1, cols, grad_step)
        send_tok[block(me, cap), cuts[c]] = grad_rows(me, c)

    def sum_copy(n, src_z, to):
        a, b, s = ((cot_col, rs_grad, cuts[n]) if n < CHUNKS else
                   (tok_col, rs_out, whole) if n == CHUNKS else
                   (slot_col, rs_slot, slice(0, slot_col.shape[1])))
        return remote(a.at[block(to, own), s], b.at[block(src_z, own), s],
                      rsend.at[n, to], rrecv.at[n, src_z], (me, to))

    def send_sums(n):
        loop(1, groups, lambda j: sum_copy(n, z, zpeer(j)).start())

    def take_sums(n, a, b, dst, s):
        total = a[block(z, own), s].astype(F32)
        for j in range(1, groups):
            sum_copy(n, zpeer(j), zpeer(j)).wait_recv()
            total = total + b[block(zpeer(j), own), s].astype(F32)
        dst[:, s] = total.astype(dst.dtype)

    loop(1, cols, lambda j: out_copy(peer(j), peer(j)).wait_recv())
    for s in cuts:
        tok_col[:, s] = jnp.dot(pick_wt_ref[...], ret_out[:, s],
                                preferred_element_type=F32).astype(BF)
    send_sums(CHUNKS)

    def slot_step(d):
        rows = block(d, cap)
        dots = jnp.sum(send_cot[rows, :].astype(F32) * ret_out[rows, :].astype(F32),
                       axis=1, keepdims=True)
        slot_rows[rows, :] = (dots * kinv_ref[rows, :]).astype(BF)

    loop(0, cols, slot_step)
    slot_col[...] = jnp.dot(pick_t_ref[...], slot_rows[...],
                            preferred_element_type=F32).astype(BF)
    send_sums(CHUNKS + 1)

    for c in range(CHUNKS):
        loop(1, cols, lambda j, c=c: grad_copy(c, peer(j), peer(j)).wait_recv())
        cot_col[:, cuts[c]] = jnp.dot(pick_t_ref[...], send_tok[:, cuts[c]],
                                      preferred_element_type=F32).astype(BF)
        send_sums(c)
    take_sums(CHUNKS, tok_col, rs_out, out_ref, whole)
    take_sums(CHUNKS + 1, slot_col, rs_slot, slot_ref, slice(0, slot_col.shape[1]))
    for c in range(CHUNKS):
        take_sums(c, cot_col, rs_grad, grad_ref, cuts[c])

    def finish(j):
        for c in range(CHUNKS):
            row_copy(1, c, me, peer(j)).wait_send()
            grad_copy(c, me, peer(j)).wait_send()
        out_copy(me, peer(j)).wait_send()

    loop(1, cols, finish)
    for n in range(CHUNKS + 2):
        loop(1, groups, lambda j, n=n: sum_copy(n, z, zpeer(j)).wait_send())


def layer(cols, groups, tokens, cotangent, pick, pick_t, pick_wt, row_w, kinv, gate_m, up_m, down_m):
    own, width = tokens.shape
    slots, col_tok = pick.shape
    ff = gate_m.shape[1]
    lanes = kinv.shape[1]
    dma = pltpu.SemaphoreType.DMA
    vmem = pl.BlockSpec(memory_space=pltpu.VMEM)
    rows = pltpu.VMEM((slots, width), BF)
    column = pltpu.VMEM((col_tok, width), BF)
    return pl.pallas_call(
        functools.partial(layer_kernel, cols, groups),
        out_shape=(
            jax.ShapeDtypeStruct((own, width), BF),
            jax.ShapeDtypeStruct((own, width), BF),
            jax.ShapeDtypeStruct((own, lanes), F32),
        ),
        in_specs=[vmem] * 10,
        out_specs=(vmem, vmem, vmem),
        scratch_shapes=[
            column, column, rows, rows, rows, rows, rows,
            pltpu.VMEM((slots, ff), BF), pltpu.VMEM((slots, ff), BF),
            pltpu.VMEM((slots, lanes), BF), pltpu.VMEM((col_tok, lanes), BF),
            column, column, pltpu.VMEM((col_tok, lanes), BF),
            dma((2, CHUNKS, groups)), dma((2, CHUNKS, groups)),
            dma((2, CHUNKS, cols)), dma((2, CHUNKS, cols)),
            dma((cols,)), dma((cols,)),
            dma((CHUNKS, cols)), dma((CHUNKS, cols)),
            dma((CHUNKS + 2, groups)), dma((CHUNKS + 2, groups)),
        ],
        compiler_params=pltpu.CompilerParams(
            collective_id=0, has_side_effects=True, vmem_limit_bytes=VMEM_BYTES),
    )(tokens, cotangent, pick, pick_t, pick_wt, row_w, kinv, gate_m, up_m, down_m)


def shards(tokens, cotangent, expert_ids, router_probs, w_gate, w_up, w_down):
    cols = lax.axis_size("expert")
    groups = lax.axis_size("dp")
    group = lax.axis_index("dp")
    own, width = tokens.shape
    col_tok, top = expert_ids.shape
    capacity = col_tok * top * 5 // (4 * cols * groups)
    piece = width // PIECES
    cuts = [slice(h * piece, (h + 1) * piece) for h in range(PIECES)]

    def exchange(rows):
        return lax.all_to_all(rows, "expert", split_axis=0, concat_axis=0, tiled=True)

    def gather(rows):
        return lax.all_gather(rows, "dp", axis=0, tiled=True)

    def scatter(rows):
        return lax.psum_scatter(rows, "dp", scatter_dimension=0, tiled=True)

    weights = router_probs / jnp.sum(router_probs, axis=1, keepdims=True)
    experts = jnp.arange(cols, dtype=jnp.int32) * groups + group
    named = expert_ids[None, :, :] == experts[:, None, None]
    hit = jnp.any(named, axis=2)
    slot_w = jnp.sum(jnp.where(named, weights[None], 0.0), axis=2)
    step = jnp.arange(col_tok, dtype=jnp.int32)
    before = (step[:, None] < step[None, :]).astype(BF)
    place = jnp.dot(hit.astype(BF), before, preferred_element_type=F32).astype(jnp.int32)
    place = jnp.where(hit, place, -1)
    pick = place[:, None, :] == jnp.arange(capacity, dtype=jnp.int32)[None, :, None]
    row_w = jnp.sum(jnp.where(pick, slot_w[:, None, :], 0.0), axis=2).reshape(-1, 1)
    pick_w = jnp.where(pick, slot_w[:, None, :], 0.0).astype(BF).reshape(cols * capacity, col_tok)
    pick = pick.astype(BF).reshape(cols * capacity, col_tok)

    own_probs = lax.dynamic_slice_in_dim(router_probs, group * own, own, 0)
    own_total = jnp.sum(own_probs, axis=1, keepdims=True)
    own_w = own_probs / own_total

    def prob_grad_of(slot_sum):
        return (slot_sum - jnp.sum(own_w * slot_sum, axis=1, keepdims=True)) / own_total

    slots = cols * capacity
    ff = w_gate.shape[2]
    held = 2 * (5 * slots * width + 4 * col_tok * width + 3 * width * ff + 2 * slots * ff)
    held = held + 6 * slots * col_tok
    if held < VMEM_BYTES:
        k_of = jnp.sum(jnp.where(named, jnp.arange(top, dtype=jnp.int32), 0), axis=2)
        row_k = jnp.sum(
            jnp.where(pick.reshape(cols, capacity, col_tok) > 0, k_of[:, None, :], 0), axis=2
        ).reshape(-1, 1)
        lanes = jnp.arange(128, dtype=jnp.int32)[None, :]
        kinv = jnp.where((row_k == lanes) & (row_w > 0), 1.0 / jnp.maximum(row_w, 1e-30), 0.0)
        out_sum, grad_sum, slot_sum = layer(
            cols, groups, tokens, cotangent, pick, pick.T, pick_w.T, row_w, kinv,
            w_gate[0], w_up[0], w_down[0])
        return out_sum, grad_sum, prob_grad_of(slot_sum[:, :top])

    tok_col = [gather(tokens[:, s]) for s in cuts]
    cot_col = [gather(cotangent[:, s]) for s in cuts]


    def select(rows):
        return jnp.dot(pick, rows, preferred_element_type=F32).astype(BF)

    def send(rows):
        return exchange(rows.reshape(cols, capacity, -1)).reshape(cols * capacity, -1)

    def combine(matrix, rows):
        return lax.dot_general(
            matrix, rows, (((0,), (0,)), ((), ())), preferred_element_type=F32
        ).astype(BF)

    gate_m, up_m, down_m = w_gate[0], w_up[0], w_down[0]
    x = [send(select(c)) for c in tok_col]
    cot_sel = [select(c) for c in cot_col]
    cot = [send((row_w * c.astype(F32)).astype(BF)) for c in cot_sel]

    gate = sum(jnp.dot(r, gate_m[s], preferred_element_type=F32) for r, s in zip(x, cuts))
    up = sum(jnp.dot(r, up_m[s], preferred_element_type=F32) for r, s in zip(x, cuts))
    sig = jax.nn.sigmoid(gate)
    hidden = (gate * sig * up).astype(BF)
    back = [
        send(jnp.dot(hidden, down_m[:, s], preferred_element_type=F32).astype(BF)) for s in cuts
    ]
    out_sum = jnp.concatenate([scatter(combine(pick_w, b)) for b in back], axis=1)

    hg = sum(
        lax.dot_general(r, down_m[:, s], NT, preferred_element_type=F32) for r, s in zip(cot, cuts)
    )
    gate_grad = (hg * up * sig * (1.0 + gate * (1.0 - sig))).astype(BF)
    up_grad = (hg * gate * sig).astype(BF)

    slot_g = sum(
        jnp.sum(c.astype(F32) * b.astype(F32), axis=1) for c, b in zip(cot_sel, back)
    ).reshape(cols, capacity)
    slot_t = jnp.sum(
        jnp.where(pick.reshape(cols, capacity, col_tok) > 0, slot_g[:, :, None], 0.0), axis=1
    )
    slot_tk = jnp.sum(jnp.where(named, slot_t[:, :, None], 0.0), axis=0)
    slot_sum = scatter(slot_tk.astype(BF)).astype(F32)

    grads = [
        send(
            (
                lax.dot_general(gate_grad, gate_m[s], NT, preferred_element_type=F32)
                + lax.dot_general(up_grad, up_m[s], NT, preferred_element_type=F32)
            ).astype(BF)
        )
        for s in cuts
    ]
    grad_sum = jnp.concatenate([scatter(combine(pick, g)) for g in grads], axis=1)

    return out_sum, grad_sum, prob_grad_of(slot_sum)


def solution(mesh):
    rows = P(("expert", "dp"), None)
    mats = P(("expert", "dp"), None, None)
    return jax.shard_map(
        shards,
        mesh=mesh,
        in_specs=(rows, rows, P("expert", None), P("expert", None), mats, mats, mats),
        out_specs=(rows, rows, rows),
        check_vma=False,
    )
```

```python
import functools

import jax
import jax.numpy as jnp
from jax import lax
from jax.experimental import pallas as pl
from jax.experimental.pallas import tpu as pltpu
from jax.sharding import PartitionSpec as P

BF = jnp.bfloat16
F32 = jnp.float32
PIECES = 2
NT = (((1,), (1,)), ((), ()))
CHUNKS = 4
VMEM_BYTES = 60 * 1024 * 1024
MESH = pl.DeviceIdType.MESH


def layer_kernel(
    cols, groups, tok_ref, cot_ref, pick_ref, pick_t_ref, pick_wt_ref, row_w_ref, kinv_ref,
    gate_ref, up_ref, down_ref, out_ref, grad_ref, slot_ref,
    tok_col, cot_col, send_tok, recv_tok, send_cot, recv_cot, ret_out, gate_keep, up_keep,
    slot_rows, slot_col, rs_out, rs_grad, rs_slot,
    zsend, zrecv, ssend, srecv, osend, orecv, gsend, grecv, rsend, rrecv,
):
    me = lax.axis_index("expert")
    z = lax.axis_index("dp")
    own, width = tok_ref.shape
    cap = pick_ref.shape[0] // cols
    part = width // CHUNKS
    cuts = [slice(c * part, (c + 1) * part) for c in range(CHUNKS)]
    whole = slice(0, width)

    def block(index, size):
        return pl.ds(pl.multiple_of(index * size, 16), size)

    def peer(j):
        return lax.rem(me + j, cols)

    def zpeer(j):
        return lax.rem(z + j, groups)

    def loop(start, stop, body):
        def step(j, carry):
            body(j)
            return carry
        lax.fori_loop(start, stop, step, 0)

    def remote(src, dst, send, recv, device):
        return pltpu.make_async_remote_copy(
            src_ref=src, dst_ref=dst, send_sem=send, recv_sem=recv,
            device_id=device, device_id_type=MESH,
        )

    barrier = pltpu.get_barrier_semaphore()
    loop(1, cols, lambda j: pl.semaphore_signal(
        barrier, inc=1, device_id=(peer(j), z), device_id_type=MESH))
    loop(1, groups, lambda j: pl.semaphore_signal(
        barrier, inc=1, device_id=(me, zpeer(j)), device_id_type=MESH))
    pl.semaphore_wait(barrier, cols + groups - 2)

    def zcopy(k, c, src_z, to):
        src = (tok_ref, cot_ref)[k]
        dst = (tok_col, cot_col)[k]
        return remote(src.at[:, cuts[c]], dst.at[block(src_z, own), cuts[c]],
                      zsend.at[k, c, to], zrecv.at[k, c, src_z], (me, to))

    def zstart(n):
        if n < 2 * CHUNKS:
            loop(1, groups, lambda j: zcopy(n // CHUNKS, n % CHUNKS, z, zpeer(j)).start())

    zstart(0)
    zstart(1)
    tok_col[block(z, own), :] = tok_ref[...]
    cot_col[block(z, own), :] = cot_ref[...]

    def row_copy(k, c, src, to):
        a = (send_tok, send_cot)[k]
        b = (recv_tok, recv_cot)[k]
        return remote(a.at[block(to, cap), cuts[c]], b.at[block(src, cap), cuts[c]],
                      ssend.at[k, c, to], srecv.at[k, c, src], (to, z))

    for k in range(2):
        for c in range(CHUNKS):
            loop(1, groups, lambda j, k=k, c=c: zcopy(k, c, zpeer(j), zpeer(j)).wait_recv())
            zstart(k * CHUNKS + c + 2)

            def picked(d, k=k, c=c):
                col = (tok_col, cot_col)[k]
                rows = jnp.dot(pick_ref[block(d, cap), :], col[:, cuts[c]],
                               preferred_element_type=F32)
                if k == 1:
                    rows = rows * row_w_ref[block(d, cap), :]
                return rows.astype(BF)

            def dispatch(j, k=k, c=c):
                d = peer(j)
                (send_tok, send_cot)[k][block(d, cap), cuts[c]] = picked(d)
                if k == 1:
                    row_copy(0, c, me, d).wait_send()
                row_copy(k, c, me, d).start()

            loop(1, cols, dispatch)
            mine = picked(me)
            (recv_tok, recv_cot)[k][block(me, cap), cuts[c]] = mine
            if k == 1:
                send_cot[block(me, cap), cuts[c]] = mine
    for k in range(2):
        for c in range(CHUNKS):
            loop(1, groups, lambda j, k=k, c=c: zcopy(k, c, z, zpeer(j)).wait_send())

    def out_copy(src, to):
        return remote(recv_tok.at[block(to, cap), :], ret_out.at[block(src, cap), :],
                      osend.at[to], orecv.at[src], (to, z))

    def forward(s):
        rows = block(s, cap)
        x = recv_tok[rows, :]
        gate = jnp.dot(x, gate_ref[...], preferred_element_type=F32)
        up = jnp.dot(x, up_ref[...], preferred_element_type=F32)
        gate_keep[rows, :] = gate.astype(BF)
        up_keep[rows, :] = up.astype(BF)
        hidden = (gate * jax.nn.sigmoid(gate) * up).astype(BF)
        return jnp.dot(hidden, down_ref[...], preferred_element_type=F32).astype(BF)

    ret_out[block(me, cap), :] = forward(me)

    def forward_step(j):
        s = peer(cols - j)
        for c in range(CHUNKS):
            row_copy(0, c, s, s).wait_recv()
        recv_tok[block(s, cap), :] = forward(s)
        out_copy(me, s).start()

    loop(1, cols, forward_step)

    def backward(s):
        rows = block(s, cap)
        hg = lax.dot_general(recv_cot[rows, :], down_ref[...], NT, preferred_element_type=F32)
        gate = gate_keep[rows, :].astype(F32)
        up = up_keep[rows, :].astype(F32)
        sig = jax.nn.sigmoid(gate)
        gate_keep[rows, :] = (hg * up * sig * (1.0 + gate * (1.0 - sig))).astype(BF)
        up_keep[rows, :] = (hg * gate * sig).astype(BF)

    backward(me)

    def backward_step(j):
        s = peer(cols - j)
        for c in range(CHUNKS):
            row_copy(1, c, s, s).wait_recv()
        backward(s)

    loop(1, cols, backward_step)

    def grad_copy(c, src, to):
        return remote(recv_cot.at[block(to, cap), cuts[c]], send_tok.at[block(src, cap), cuts[c]],
                      gsend.at[c, to], grecv.at[c, src], (to, z))

    def grad_rows(s, c):
        rows = block(s, cap)
        return (
            lax.dot_general(gate_keep[rows, :], gate_ref[cuts[c], :], NT,
                            preferred_element_type=F32)
            + lax.dot_general(up_keep[rows, :], up_ref[cuts[c], :], NT,
                              preferred_element_type=F32)
        ).astype(BF)

    for c in range(CHUNKS):
        def grad_step(j, c=c):
            s = peer(cols - j)
            recv_cot[block(s, cap), cuts[c]] = grad_rows(s, c)
            grad_copy(c, me, s).start()

        loop(1, cols, grad_step)
        send_tok[block(me, cap), cuts[c]] = grad_rows(me, c)

    def sum_copy(n, src_z, to):
        a, b, s = ((cot_col, rs_grad, cuts[n]) if n < CHUNKS else
                   (tok_col, rs_out, whole) if n == CHUNKS else
                   (slot_col, rs_slot, slice(0, slot_col.shape[1])))
        return remote(a.at[block(to, own), s], b.at[block(src_z, own), s],
                      rsend.at[n, to], rrecv.at[n, src_z], (me, to))

    def send_sums(n):
        loop(1, groups, lambda j: sum_copy(n, z, zpeer(j)).start())

    def take_sums(n, a, b, dst, s):
        total = a[block(z, own), s].astype(F32)
        for j in range(1, groups):
            sum_copy(n, zpeer(j), zpeer(j)).wait_recv()
            total = total + b[block(zpeer(j), own), s].astype(F32)
        dst[:, s] = total.astype(dst.dtype)

    loop(1, cols, lambda j: out_copy(peer(j), peer(j)).wait_recv())
    for s in cuts:
        tok_col[:, s] = jnp.dot(pick_wt_ref[...], ret_out[:, s],
                                preferred_element_type=F32).astype(BF)
    send_sums(CHUNKS)

    def slot_step(d):
        rows = block(d, cap)
        dots = jnp.sum(send_cot[rows, :].astype(F32) * ret_out[rows, :].astype(F32),
                       axis=1, keepdims=True)
        slot_rows[rows, :] = (dots * kinv_ref[rows, :]).astype(BF)

    loop(0, cols, slot_step)
    slot_col[...] = jnp.dot(pick_t_ref[...], slot_rows[...],
                            preferred_element_type=F32).astype(BF)
    send_sums(CHUNKS + 1)

    for c in range(CHUNKS):
        loop(1, cols, lambda j, c=c: grad_copy(c, peer(j), peer(j)).wait_recv())
        cot_col[:, cuts[c]] = jnp.dot(pick_t_ref[...], send_tok[:, cuts[c]],
                                      preferred_element_type=F32).astype(BF)
        send_sums(c)
    take_sums(CHUNKS, tok_col, rs_out, out_ref, whole)
    take_sums(CHUNKS + 1, slot_col, rs_slot, slot_ref, slice(0, slot_col.shape[1]))
    for c in range(CHUNKS):
        take_sums(c, cot_col, rs_grad, grad_ref, cuts[c])

    def finish(j):
        for c in range(CHUNKS):
            row_copy(1, c, me, peer(j)).wait_send()
            grad_copy(c, me, peer(j)).wait_send()
        out_copy(me, peer(j)).wait_send()

    loop(1, cols, finish)
    for n in range(CHUNKS + 2):
        loop(1, groups, lambda j, n=n: sum_copy(n, z, zpeer(j)).wait_send())


def layer(cols, groups, tokens, cotangent, pick, pick_t, pick_wt, row_w, kinv, gate_m, up_m, down_m):
    own, width = tokens.shape
    slots, col_tok = pick.shape
    ff = gate_m.shape[1]
    lanes = kinv.shape[1]
    dma = pltpu.SemaphoreType.DMA
    vmem = pl.BlockSpec(memory_space=pltpu.VMEM)
    rows = pltpu.VMEM((slots, width), BF)
    column = pltpu.VMEM((col_tok, width), BF)
    return pl.pallas_call(
        functools.partial(layer_kernel, cols, groups),
        out_shape=(
            jax.ShapeDtypeStruct((own, width), BF),
            jax.ShapeDtypeStruct((own, width), BF),
            jax.ShapeDtypeStruct((own, lanes), F32),
        ),
        in_specs=[vmem] * 10,
        out_specs=(vmem, vmem, vmem),
        scratch_shapes=[
            column, column, rows, rows, rows, rows, rows,
            pltpu.VMEM((slots, ff), BF), pltpu.VMEM((slots, ff), BF),
            pltpu.VMEM((slots, lanes), BF), pltpu.VMEM((col_tok, lanes), BF),
            column, column, pltpu.VMEM((col_tok, lanes), BF),
            dma((2, CHUNKS, groups)), dma((2, CHUNKS, groups)),
            dma((2, CHUNKS, cols)), dma((2, CHUNKS, cols)),
            dma((cols,)), dma((cols,)),
            dma((CHUNKS, cols)), dma((CHUNKS, cols)),
            dma((CHUNKS + 2, groups)), dma((CHUNKS + 2, groups)),
        ],
        compiler_params=pltpu.CompilerParams(
            collective_id=0, has_side_effects=True, vmem_limit_bytes=VMEM_BYTES),
    )(tokens, cotangent, pick, pick_t, pick_wt, row_w, kinv, gate_m, up_m, down_m)


def shards(tokens, cotangent, expert_ids, router_probs, w_gate, w_up, w_down):
    cols = lax.axis_size("expert")
    groups = lax.axis_size("dp")
    group = lax.axis_index("dp")
    own, width = tokens.shape
    col_tok, top = expert_ids.shape
    capacity = col_tok * top * 5 // (4 * cols * groups)
    piece = width // PIECES
    cuts = [slice(h * piece, (h + 1) * piece) for h in range(PIECES)]

    def exchange(rows):
        return lax.all_to_all(rows, "expert", split_axis=0, concat_axis=0, tiled=True)

    def gather(rows):
        return lax.all_gather(rows, "dp", axis=0, tiled=True)

    def scatter(rows):
        return lax.psum_scatter(rows, "dp", scatter_dimension=0, tiled=True)

    weights = router_probs / jnp.sum(router_probs, axis=1, keepdims=True)
    experts = jnp.arange(cols, dtype=jnp.int32) * groups + group
    named = expert_ids[None, :, :] == experts[:, None, None]
    hit = jnp.any(named, axis=2)
    slot_w = jnp.sum(jnp.where(named, weights[None], 0.0), axis=2)
    step = jnp.arange(col_tok, dtype=jnp.int32)
    before = (step[:, None] < step[None, :]).astype(BF)
    place = jnp.dot(hit.astype(BF), before, preferred_element_type=F32).astype(jnp.int32)
    place = jnp.where(hit, place, -1)
    pick = place[:, None, :] == jnp.arange(capacity, dtype=jnp.int32)[None, :, None]
    row_w = jnp.sum(jnp.where(pick, slot_w[:, None, :], 0.0), axis=2).reshape(-1, 1)
    pick_w = jnp.where(pick, slot_w[:, None, :], 0.0).astype(BF).reshape(cols * capacity, col_tok)
    pick = pick.astype(BF).reshape(cols * capacity, col_tok)

    own_probs = lax.dynamic_slice_in_dim(router_probs, group * own, own, 0)
    own_total = jnp.sum(own_probs, axis=1, keepdims=True)
    own_w = own_probs / own_total

    def prob_grad_of(slot_sum):
        return (slot_sum - jnp.sum(own_w * slot_sum, axis=1, keepdims=True)) / own_total

    slots = cols * capacity
    ff = w_gate.shape[2]
    held = 2 * (5 * slots * width + 4 * col_tok * width + 3 * width * ff + 2 * slots * ff)
    held = held + 6 * slots * col_tok
    if held < VMEM_BYTES:
        k_of = jnp.sum(jnp.where(named, jnp.arange(top, dtype=jnp.int32), 0), axis=2)
        row_k = jnp.sum(
            jnp.where(pick.reshape(cols, capacity, col_tok) > 0, k_of[:, None, :], 0), axis=2
        ).reshape(-1, 1)
        lanes = jnp.arange(128, dtype=jnp.int32)[None, :]
        kinv = jnp.where((row_k == lanes) & (row_w > 0), 1.0 / jnp.maximum(row_w, 1e-30), 0.0)
        out_sum, grad_sum, slot_sum = layer(
            cols, groups, tokens, cotangent, pick, pick.T, pick_w.T, row_w, kinv,
            w_gate[0], w_up[0], w_down[0])
        return out_sum, grad_sum, prob_grad_of(slot_sum[:, :top])

    tok_col = [gather(tokens[:, s]) for s in cuts]
    cot_col = [gather(cotangent[:, s]) for s in cuts]


    def select(rows):
        return jnp.dot(pick, rows, preferred_element_type=F32).astype(BF)

    def send(rows):
        return exchange(rows.reshape(cols, capacity, -1)).reshape(cols * capacity, -1)

    def combine(matrix, rows):
        return lax.dot_general(
            matrix, rows, (((0,), (0,)), ((), ())), preferred_element_type=F32
        ).astype(BF)

    gate_m, up_m, down_m = w_gate[0], w_up[0], w_down[0]
    x = [send(select(c)) for c in tok_col]
    cot_sel = [select(c) for c in cot_col]
    cot = [send((row_w * c.astype(F32)).astype(BF)) for c in cot_sel]

    gate = sum(jnp.dot(r, gate_m[s], preferred_element_type=F32) for r, s in zip(x, cuts))
    up = sum(jnp.dot(r, up_m[s], preferred_element_type=F32) for r, s in zip(x, cuts))
    sig = jax.nn.sigmoid(gate)
    hidden = (gate * sig * up).astype(BF)
    back = [
        send(jnp.dot(hidden, down_m[:, s], preferred_element_type=F32).astype(BF)) for s in cuts
    ]
    out_sum = jnp.concatenate([scatter(combine(pick_w, b)) for b in back], axis=1)

    hg = sum(
        lax.dot_general(r, down_m[:, s], NT, preferred_element_type=F32) for r, s in zip(cot, cuts)
    )
    gate_grad = (hg * up * sig * (1.0 + gate * (1.0 - sig))).astype(BF)
    up_grad = (hg * gate * sig).astype(BF)

    slot_g = sum(
        jnp.sum(c.astype(F32) * b.astype(F32), axis=1) for c, b in zip(cot_sel, back)
    ).reshape(cols, capacity)
    slot_t = jnp.sum(
        jnp.where(pick.reshape(cols, capacity, col_tok) > 0, slot_g[:, :, None], 0.0), axis=1
    )
    slot_tk = jnp.sum(jnp.where(named, slot_t[:, :, None], 0.0), axis=0)
    slot_sum = scatter(slot_tk.astype(BF)).astype(F32)

    grads = [
        send(
            (
                lax.dot_general(gate_grad, gate_m[s], NT, preferred_element_type=F32)
                + lax.dot_general(up_grad, up_m[s], NT, preferred_element_type=F32)
            ).astype(BF)
        )
        for s in cuts
    ]
    grad_sum = jnp.concatenate([scatter(combine(pick, g)) for g in grads], axis=1)

    return out_sum, grad_sum, prob_grad_of(slot_sum)


def solution(mesh):
    rows = P(("expert", "dp"), None)
    mats = P(("expert", "dp"), None, None)
    return jax.shard_map(
        shards,
        mesh=mesh,
        in_specs=(rows, rows, P("expert", None), P("expert", None), mats, mats, mats),
        out_specs=(rows, rows, rows),
        check_vma=False,
    )
```
